32 devices in a mesh: ctx: 8 (over z, y), head: 4 (over x, core).
Axes of the slice: x: 2, y: 2, z: 4, core: 2. Of those that a mesh axis runs over, the one named last changes fastest.
Arguments:
- queries: bfloat16 [32, 8192, 128], P('head', 'ctx'), may hold values from -0.52734375 to 0.52734375
- key_rows: bfloat16 [32, 8192, 128], P('head', 'ctx'), may hold values from -0.52734375 to 0.52734375
- value_rows: bfloat16 [32, 8192, 128], P('head', 'ctx'), may hold values from -0.52734375 to 0.52734375
- level_weight: float32 [4, 8192], P(None, 'ctx'), may hold values from 0.2 to 2
- out_grad: bfloat16 [32, 8192, 128], P('head', 'ctx'), may hold values from -1.0546875 to 1.0546875
Outputs:
- query_grad: bfloat16 [32, 8192, 128], P('head', 'ctx')
- key_grad: bfloat16 [32, 8192, 128], P('head', 'ctx')
- value_grad: bfloat16 [32, 8192, 128], P('head', 'ctx')
- weight_grad: float32 [4, 8192], P(None, 'ctx')
The draws below stay inside these ranges and needn't reach their ends.
All inputs are finite; a program needn't handle non-finite values.
Results may differ from the reference program's by a relative error of at most 0.0057.
Values sent between devices are 32-bit elements; how exact they have to be, the bound alone decides.
No kernel may reach another device: no remote copies, remote signals or barrier semaphores. Data moves between devices by JAX's collectives and lax.ppermute only.
A program may use at most 128 MiB of HBM per device.

```python
import math
import jax
import jax.numpy as jnp
import numpy as np
from jax import lax

H = 32
DH = 128
TOK_DEV = 1024
TOKENS = 8192
LEVELS = 3
N_CTX = 8


def steps_of(key, shape, cuts, low, largest):
    factor_of, own = 1.0, jax.random.fold_in(key, 6)
    for position, parts in cuts:
        heights = jnp.exp(jax.random.uniform(jax.random.fold_in(own, position), (parts,), jnp.float32, low / len(cuts), largest / len(cuts)))
        factor_of = factor_of * jnp.repeat(heights, shape[position] // parts).reshape([-1 if axis == position else 1 for axis in range(len(shape))])
    return factor_of


def gaussian(key, dims, width, limit, shards=(), kind=jnp.bfloat16):
    values = width * jax.random.normal(key, dims, jnp.float32)
    if shards:
        values = values * steps_of(key, dims, shards, -0.22, 0.18)
    return jnp.clip(values, -limit, limit).astype(kind)


def setup_inputs(seed: int = 0) -> dict:
    keys = jax.random.split(jax.random.key(seed), 6)
    queries = gaussian(keys[0], (H, TOKENS, DH), (DH ** -0.5), 0.52734375, ((0, 4), (1, 8)))
    key_rows = gaussian(keys[1], (H, TOKENS, DH), (DH ** -0.5), 0.52734375, ((0, 4), (1, 8)))
    value_rows = gaussian(keys[2], (H, TOKENS, DH), (DH ** -0.5), 0.52734375, ((0, 4), (1, 8)))
    level_weight = jnp.clip(jnp.exp(math.log(2.0) - 2.3025851 * jax.random.uniform(keys[3], (LEVELS + 1, TOKENS), jnp.float32) ** steps_of(keys[3], (LEVELS + 1, TOKENS), ((1, 8),), -0.2, 0.2)), 0.2, 2.0)
    out_grad = gaussian(keys[4], (H, TOKENS, DH), ((2 * DH / TOKENS) ** 0.5), 1.0546875, ((0, 4), (1, 8)))
    return dict(queries=queries, key_rows=key_rows, value_rows=value_rows, level_weight=level_weight, out_grad=out_grad)


highest = lax.Precision.HIGHEST


def as_float(array):
    return array.astype(jnp.float32)


def head_part(operands, weights, flag_rows):
    queries, key_rows, value_rows, out_grad, states = operands
    q_f = as_float(queries)
    k_f = as_float(key_rows)
    v_f = as_float(value_rows)
    g_f = as_float(out_grad)
    steps = jnp.arange(TOK_DEV, dtype=jnp.int32)
    causal = (steps[:, None] >= steps[None, :]).astype(jnp.float32)
    scale = causal[None] * weights[0][:, :, None]
    raw = jnp.einsum('ntd,nsd->nts', q_f, k_f, precision=highest)
    attn = (scale * raw).astype(jnp.bfloat16)
    d_attn = jnp.einsum('ntd,nsd->nts', g_f, v_f, precision=highest)
    local_weight = jnp.sum(causal[None] * raw * d_attn, axis=2)
    d_raw = as_float((scale * d_attn).astype(jnp.bfloat16))
    local_q = jnp.einsum('nts,nsd->ntd', d_raw, k_f, precision=highest)
    local_k = jnp.einsum('nts,ntd->nsd', d_raw, q_f, precision=highest)
    local_v = jnp.einsum('nts,ntd->nsd', as_float(attn), g_f, precision=highest)
    z_all = jnp.einsum('nte,lnde->lntd', g_f, as_float(states), precision=highest)
    query_sum = local_q + jnp.sum(weights[1:][:, :, :, None] * z_all, axis=0)
    level_weights = jnp.sum(z_all * q_f[None], axis=3)
    weighted = as_float((weights[1:][:, :, :, None] * g_f[None]).astype(jnp.bfloat16))
    state_grad = jnp.einsum('ntd,lnte->lnde', q_f, weighted, precision=highest)
    state_grad = state_grad * flag_rows[:, :, None, None]
    weight_rows = jnp.concatenate([local_weight[None], level_weights], axis=0)
    return query_sum, local_k, local_v, weight_rows, state_grad


def reference(queries, key_rows, value_rows, level_weight, out_grad):
    def shaped(array):
        return array.reshape(H, N_CTX, TOK_DEV, DH)

    q_all, k_all, v_all, g_all = shaped(queries), shaped(key_rows), shaped(value_rows), shaped(out_grad)
    weights = level_weight.reshape(LEVELS + 1, N_CTX, TOK_DEV)
    group_state = jnp.einsum('hntd,hnte->hnde', as_float(k_all), as_float(v_all), precision=highest)
    positions = np.arange(N_CTX)
    states = []
    flag_list = []
    siblings = []
    for height in range(LEVELS):
        span = 2 ** height
        sums = group_state.reshape(H, N_CTX // span, span, DH, DH).sum(axis=2)
        parity = jnp.asarray((positions // span) % 2, dtype=jnp.float32)
        sibling = (positions // span) ^ 1
        siblings.append(sibling)
        flag_list.append(parity)
        states.append(sums[:, sibling] * parity[None, :, None, None])
    state_bf = jnp.stack(states, axis=1).astype(jnp.bfloat16)
    flag_rows = jnp.stack(flag_list, axis=0)

    def one_head(operands):
        return head_part(operands, weights, flag_rows)

    query_sum, local_k, local_v, weight_rows, state_grad = lax.map(
        one_head, (q_all, k_all, v_all, g_all, state_bf))
    group_grad = jnp.zeros((H, N_CTX, DH, DH), jnp.float32)
    for height in range(LEVELS):
        span = 2 ** height
        sums = state_grad[:, height].reshape(H, N_CTX // span, span, DH, DH).sum(axis=2)
        clear = 1.0 - flag_list[height]
        group_grad = group_grad + sums[:, siblings[height]] * clear[None, :, None, None]
    grad_bf = as_float(group_grad.astype(jnp.bfloat16))
    key_sum = local_k + jnp.einsum('hnse,hnde->hnsd', as_float(v_all), grad_bf, precision=highest)
    value_sum = local_v + jnp.einsum('hnsd,hnde->hnse', as_float(k_all), grad_bf, precision=highest)
    query_grad = query_sum.astype(jnp.bfloat16).reshape(H, N_CTX * TOK_DEV, DH)
    key_grad = key_sum.astype(jnp.bfloat16).reshape(H, N_CTX * TOK_DEV, DH)
    value_grad = value_sum.astype(jnp.bfloat16).reshape(H, N_CTX * TOK_DEV, DH)
    weight_grad = jnp.sum(weight_rows, axis=0).reshape(LEVELS + 1, N_CTX * TOK_DEV)
    return query_grad, key_grad, value_grad, weight_grad
```

```python
import jax
import jax.numpy as jnp
from jax import lax
from jax.experimental import pallas as pl
from jax.experimental.pallas import tpu as pltpu
from jax.sharding import PartitionSpec as P

F32, BF16 = jnp.float32, jnp.bfloat16
NN = (((1,), (0,)), ((), ()))
NT = (((1,), (1,)), ((), ()))
TN = (((0,), (0,)), ((), ()))
VMEM_BYTES = 40 * 2**20
PARTS = 2
GROUPS = (2, 1, 1, 2, 1, 1)


def dot(a, b, dims):
    return lax.dot_general(a, b, dims, preferred_element_type=F32)


def any_spec():
    return pl.BlockSpec(memory_space=pl.ANY)


def smem_spec():
    return pl.BlockSpec(memory_space=pltpu.SMEM)


def head_spec(shape, first):
    return pl.BlockSpec((1,) + shape[1:], lambda h: (first + h, 0, 0))


def params():
    return pltpu.CompilerParams(vmem_limit_bytes=VMEM_BYTES)


def cost(flops, bytes_accessed):
    return pl.CostEstimate(flops=int(flops), bytes_accessed=int(bytes_accessed), transcendentals=0)


def states_of(key_rows, value_rows, first, count, deps):
    _, length, depth = key_rows.shape

    def kernel(k_ref, v_ref, *rest):
        rest[-1][0] = dot(k_ref[0], v_ref[0], TN)

    return pl.pallas_call(
        kernel,
        grid=(count,),
        in_specs=[head_spec(key_rows.shape, first)] * 2 + [any_spec()] * len(deps),
        out_specs=pl.BlockSpec((1, depth, depth), lambda h: (h, 0, 0)),
        out_shape=jax.ShapeDtypeStruct((count, depth, depth), F32),
        compiler_params=params(),
        cost_estimate=cost(count * length * depth * depth * 8, count * length * depth * 4),
        name="states",
    )(key_rows, value_rows, *deps)


def state_grads_of(flags, queries, out_grad, level_weight, first, count, deps):
    _, length, depth = queries.shape
    levels = level_weight.shape[0] - 1

    def kernel(flag_ref, q_ref, g_ref, w_ref, *rest):
        outs, columns = rest[len(deps) : len(deps) + levels], rest[-1]

        @pl.when(pl.program_id(0) == 0)
        def _():
            for level in range(levels):
                row = w_ref[level + 1 : level + 2, :] * flag_ref[level]
                columns[level] = jnp.broadcast_to(row, (depth, length)).T

        g = g_ref[0].astype(F32)
        weighted = [(columns[level] * g).astype(BF16) for level in range(levels)]
        grads = dot(q_ref[0], jnp.concatenate(weighted, axis=1), TN)
        for level in range(levels):
            outs[level][0] = grads[:, level * depth : (level + 1) * depth]

    return pl.pallas_call(
        kernel,
        grid=(count,),
        in_specs=[smem_spec()]
        + [head_spec(queries.shape, first)] * 2
        + [pl.BlockSpec(level_weight.shape, lambda h: (0, 0))]
        + [any_spec()] * len(deps),
        out_specs=[pl.BlockSpec((1, depth, depth), lambda h: (h, 0, 0))] * levels,
        out_shape=[jax.ShapeDtypeStruct((count, depth, depth), F32)] * levels,
        scratch_shapes=[pltpu.VMEM((levels, length, depth), F32)],
        compiler_params=params(),
        cost_estimate=cost(
            levels * count * length * depth * depth * 8, count * length * depth * 4
        ),
        name="state_grads",
    )(flags, queries, out_grad, level_weight, *deps)


def local_of(level_weight, queries, key_rows, value_rows, out_grad, held, first, count, deps):
    heads, length, depth = queries.shape
    tile = min(256, length)

    def kernel(w_ref, q_ref, k_ref, v_ref, g_ref, *rest):
        lq_ref, lk_ref, lv_ref, lw_ref, k_sum, v_sum = rest[-6:]

        @pl.when(pl.program_id(0) == 0)
        def _():
            lw_ref[...] = jnp.zeros_like(lw_ref)

        k_turned = k_ref[0].T
        for i in range(length // tile):
            upto = (i + 1) * tile
            t = pl.ds(i * tile, tile)
            s = pl.ds(0, upto)
            q, g, w = q_ref[0, t, :], g_ref[0, t, :], w_ref[0:1, t]
            raw = dot(k_ref[0, s, :], q, NT)
            d_attn = dot(v_ref[0, s, :], g, NT)
            rows = lax.broadcasted_iota(jnp.int32, (upto, tile), 0)
            columns = lax.broadcasted_iota(jnp.int32, (upto, tile), 1) + i * tile
            raw = jnp.where(rows <= columns, raw, 0.0)
            d_attn = jnp.where(rows <= columns, d_attn, 0.0)
            lw_ref[0:1, t] += jnp.sum(raw * d_attn, axis=0, keepdims=True)
            attn = (raw * w).astype(BF16)
            d_raw = (d_attn * w).astype(BF16)
            k_part, v_part = dot(d_raw, q, NN), dot(attn, g, NN)
            k_sum[t, :] = k_part[i * tile :]
            v_sum[t, :] = v_part[i * tile :]
            if i:
                before = pl.ds(0, i * tile)
                k_sum[before, :] += k_part[: i * tile]
                v_sum[before, :] += v_part[: i * tile]
            lq_ref[0, t, :] = dot(k_turned[:, :upto], d_raw, NN).T
        lk_ref[0] = k_sum[...]
        lv_ref[0] = v_sum[...]

    spec = head_spec(queries.shape, first)
    extra = list(held) + list(deps)
    return pl.pallas_call(
        kernel,
        grid=(count,),
        in_specs=[pl.BlockSpec(level_weight.shape, lambda h: (0, 0))]
        + [spec] * 4
        + [any_spec()] * len(extra),
        out_specs=[spec] * 3 + [pl.BlockSpec((1, length), lambda h: (0, 0))],
        out_shape=[jax.ShapeDtypeStruct(queries.shape, F32)] * 3
        + [jax.ShapeDtypeStruct((1, length), F32)],
        scratch_shapes=[pltpu.VMEM((length, depth), F32)] * 2,
        input_output_aliases={5 + i: i for i in range(len(held))},
        compiler_params=params(),
        cost_estimate=cost(count * length * length * depth * 10, count * length * depth * 20),
        name="local",
    )(level_weight, queries, key_rows, value_rows, out_grad, *extra)


def query_side(flags, level_weight, queries, out_grad, sums, states, levels_here, held, kind, first, deps):
    _, length, depth = queries.shape
    number = len(levels_here)
    count = states[0][0].shape[0]
    flat = [part for parts in states for part in parts]

    def kernel(flag_ref, w_ref, q_ref, g_ref, sum_ref, *rest):
        out_ref, row_ref, columns, total = rest[-4:]

        @pl.when(pl.program_id(0) == 0)
        def _():
            for i, level in enumerate(levels_here):
                row = w_ref[level + 1 : level + 2, :]
                columns[i] = jnp.broadcast_to(row, (depth, length)).T
            total[...] = jnp.zeros_like(total)

        q, g = q_ref[0].astype(F32), g_ref[0]
        acc = sum_ref[0].astype(F32)
        at = 0
        for i, level in enumerate(levels_here):
            state = rest[at][0]
            for part in range(1, len(states[i])):
                state = state + rest[at + part][0]
            at += len(states[i])
            z = dot(g, (state * flag_ref[level]).astype(BF16), NT)
            acc += columns[i] * z
            total[i] += q * z
        out_ref[0] = acc.astype(kind)

        @pl.when(pl.program_id(0) == count - 1)
        def _():
            for i in range(number):
                row_ref[i : i + 1, :] = jnp.sum(total[i].T, axis=0, keepdims=True)

    spec = head_spec(queries.shape, first)
    small = pl.BlockSpec((1, depth, depth), lambda h: (h, 0, 0))
    extra = list(held) + list(deps)
    before = 5 + len(flat)
    aliases = {before: 0} if held else {}
    if not held and kind == sums.dtype:
        aliases = {4: 0}
    return pl.pallas_call(
        kernel,
        grid=(count,),
        in_specs=[smem_spec(), pl.BlockSpec(level_weight.shape, lambda h: (0, 0))]
        + [spec] * 3
        + [small] * len(flat)
        + [any_spec()] * len(extra),
        out_specs=[spec, pl.BlockSpec((number, length), lambda h: (0, 0))],
        out_shape=[
            jax.ShapeDtypeStruct(queries.shape, kind),
            jax.ShapeDtypeStruct((number, length), F32),
        ],
        scratch_shapes=[pltpu.VMEM((number, length, depth), F32)] * 2,
        input_output_aliases=aliases,
        compiler_params=params(),
        cost_estimate=cost(
            number * count * length * depth * depth * 8, count * length * depth * 12
        ),
        name="query_side",
    )(flags, level_weight, queries, out_grad, sums, *flat, *extra)


def key_side(key_rows, value_rows, key_sum, value_sum, parts, held, first, deps):
    _, length, depth = key_rows.shape
    count = parts[0].shape[0]

    def kernel(k_ref, v_ref, ks_ref, vs_ref, *rest):
        k_out, v_out = rest[-2:]
        grad = rest[0][0]
        for part in range(1, len(parts)):
            grad = grad + rest[part][0]
        grad = grad.astype(BF16)
        k_out[0] = (ks_ref[0] + dot(v_ref[0], grad, NT)).astype(BF16)
        v_out[0] = (vs_ref[0] + dot(k_ref[0], grad, NN)).astype(BF16)

    spec = head_spec(key_rows.shape, first)
    small = pl.BlockSpec((1, depth, depth), lambda h: (h, 0, 0))
    extra = list(held) + list(deps)
    before = 4 + len(parts)
    return pl.pallas_call(
        kernel,
        grid=(count,),
        in_specs=[spec] * 4 + [small] * len(parts) + [any_spec()] * len(extra),
        out_specs=[spec] * 2,
        out_shape=[jax.ShapeDtypeStruct(key_rows.shape, BF16)] * 2,
        input_output_aliases={before + i: i for i in range(len(held))},
        compiler_params=params(),
        cost_estimate=cost(count * length * depth * depth * 16, count * length * depth * 16),
        name="key_side",
    )(key_rows, value_rows, key_sum, value_sum, *parts, *extra)


def bit(n, level):
    return n >> level & 1


def state_steps(size, state):
    levels = size.bit_length() - 1
    states = []
    for level in range(levels):
        span = 2**level
        if level == levels - 1 and level >= 1:
            hop = span // 2
            near = [(n, n + hop) for n in range(size) if not bit(n, level) and bit(n, level - 1)]
            far = [(n, n + hop) for n in range(size) if bit(n, level) and not bit(n, level - 1)]
            first = lax.ppermute(state, "ctx", near)
            yield states, first
            second = lax.ppermute(first, "ctx", far)
            states = states + [[first, second]]
            yield states, second
        else:
            if level >= levels - 2:
                pairs = [(n, n + span) for n in range(size) if not bit(n, level)]
            else:
                pairs = [(n, n ^ span) for n in range(size)]
            got = lax.ppermute(state, "ctx", pairs)
            states = states + [[got]]
            if level < levels - 1:
                state = state + got
            yield states, got


def grad_steps(size, grads):
    levels = size.bit_length() - 1
    total = None
    for level in reversed(range(levels)):
        span = 2**level
        if level == levels - 1 and level >= 1:
            hop = span // 2
            far = [(n, n - hop) for n in range(size) if bit(n, level) and bit(n, level - 1)]
            near = [(n, n - hop) for n in range(size) if bit(n, level) and not bit(n, level - 1)]
            got = lax.ppermute(grads[level], "ctx", far)
            yield None, got
            total = lax.ppermute(grads[level] + got, "ctx", near)
            parts = [total]
            yield parts, total
        else:
            if level >= levels - 2:
                pairs = [(n, n - span) for n in range(size) if bit(n, level)]
            else:
                pairs = [(n, n ^ span) for n in range(size)]
            sent = grads[level] if total is None else grads[level] + total
            got = lax.ppermute(sent, "ctx", pairs)
            parts = [got] if total is None else [total, got]
            if level:
                total = got if total is None else total + got
            yield parts, got


def per_device(queries, key_rows, value_rows, level_weight, out_grad):
    size = lax.axis_size("ctx")
    levels = size.bit_length() - 1
    heads, length, depth = queries.shape
    position = lax.axis_index("ctx")
    flags = (position // 2 ** jnp.arange(levels, dtype=jnp.int32) % 2).astype(F32)
    parts = PARTS if heads % PARTS == 0 else 1
    count = heads // parts
    firsts = [part * count for part in range(parts)]
    ups, downs = [], []
    for first in firsts:
        ups.append(state_steps(size, states_of(key_rows, value_rows, first, count, [])))
    for first in firsts:
        grads = state_grads_of(flags, queries, out_grad, level_weight, first, count, [])
        downs.append(grad_steps(size, grads))
    groups = GROUPS if sum(GROUPS) == heads else (1,) * heads
    held, rows, start = [], [], 0
    up_state, down_state = [None] * parts, [None] * parts
    deps = []
    pending = list(groups)
    for step in range(levels + 1 if levels > 1 else levels):
        for part in range(parts):
            if pending:
                many = pending.pop(0)
                *held, row = local_of(
                    level_weight, queries, key_rows, value_rows, out_grad, held, start, many, deps
                )
                rows.append(row)
                start += many
            up_state[part], up_dep = next(ups[part])
            down_state[part], down_dep = next(downs[part])
            deps = [up_dep, down_dep]
    while pending:
        many = pending.pop(0)
        *held, row = local_of(
            level_weight, queries, key_rows, value_rows, out_grad, held, start, many, []
        )
        rows.append(row)
        start += many
    query_sum, key_sum, value_sum = held
    weight_row = sum(rows)
    level_rows = None
    query_out, key_out = [], []
    for part in range(parts):
        grad, some = query_side(
            flags,
            level_weight,
            queries,
            out_grad,
            query_sum,
            up_state[part],
            list(range(levels)),
            query_out,
            BF16,
            firsts[part],
            [],
        )
        query_out = [grad]
        level_rows = some if level_rows is None else level_rows + some
    weight_grad = jnp.concatenate([weight_row, level_rows], axis=0)
    ways = lax.axis_size("head")
    others = [
        lax.ppermute(weight_grad, "head", [(n, (n + shift) % ways) for n in range(ways)])
        for shift in range(1, ways)
    ]
    for other in others:
        weight_grad = weight_grad + other
    for part in range(parts):
        key_out = key_side(
            key_rows, value_rows, key_sum, value_sum, down_state[part], key_out, firsts[part], []
        )
    return query_out[0], key_out[0], key_out[1], weight_grad


def solution(mesh):
    placed = (
        P("head", "ctx", None),
        P("head", "ctx", None),
        P("head", "ctx", None),
        P(None, "ctx"),
        P("head", "ctx", None),
    )
    return jax.shard_map(
        per_device,
        mesh=mesh,
        in_specs=placed,
        out_specs=(
            P("head", "ctx", None),
            P("head", "ctx", None),
            P("head", "ctx", None),
            P(None, "ctx"),
        ),
        check_vma=False,
    )
```

```python
import jax
import jax.numpy as jnp
from jax import lax
from jax.experimental import pallas as pl
from jax.experimental.pallas import tpu as pltpu
from jax.sharding import PartitionSpec as P

F32, BF16 = jnp.float32, jnp.bfloat16
NN = (((1,), (0,)), ((), ()))
NT = (((1,), (1,)), ((), ()))
TN = (((0,), (0,)), ((), ()))
VMEM_BYTES = 16 * 2**20
PARTS = (4, 4)
FILL = (1, 2, 1, 1, 1, 1, 1)

INSIDE = pl.BlockSpec(memory_space=pltpu.VMEM)
OUTSIDE = pl.BlockSpec(memory_space=pltpu.HBM)
SCALARS = pl.BlockSpec(memory_space=pltpu.SMEM)
ANYWHERE = pl.BlockSpec(memory_space=pl.ANY)


def dot(a, b, dims):
    return lax.dot_general(a, b, dims, preferred_element_type=F32)


def call(kernel, name, args, specs, outs, out_specs, deps=(), aliases=None, scratch=(), flops=0):
    deps = list(deps)
    count = len(args)

    def body(*refs):
        kernel(*refs[:count], *refs[count + len(deps) :])

    return pl.pallas_call(
        body,
        in_specs=list(specs) + [ANYWHERE] * len(deps),
        out_specs=list(out_specs),
        out_shape=list(outs),
        scratch_shapes=list(scratch),
        input_output_aliases=aliases or {},
        compiler_params=pltpu.CompilerParams(vmem_limit_bytes=VMEM_BYTES),
        cost_estimate=pl.CostEstimate(flops=1, bytes_accessed=1, transcendentals=0),
        name=name,
    )(*args, *deps)


def load_states(key_rows, value_rows, held, first, count, deps):
    shape = key_rows.shape
    depth = shape[2]

    def kernel(k_hbm, v_hbm, *rest):
        k_in, v_in, state, sems = rest[-4:]
        copies = []
        for i in range(count):
            at = first + i
            copies.append(
                (
                    pltpu.make_async_copy(k_hbm.at[at], k_in.at[at], sems.at[0, i]),
                    pltpu.make_async_copy(v_hbm.at[at], v_in.at[at], sems.at[1, i]),
                )
            )
        for pair in copies:
            for copy in pair:
                copy.start()
        for i in range(count):
            for copy in copies[i]:
                copy.wait()
            state[i] = dot(k_in[first + i], v_in[first + i], TN)

    kind = pltpu.VMEM(shape, BF16)
    return call(
        kernel,
        "load_states",
        [key_rows, value_rows, *held],
        [OUTSIDE, OUTSIDE] + [INSIDE] * len(held),
        [kind, kind, jax.ShapeDtypeStruct((count, depth, depth), F32)],
        [INSIDE] * 3,
        deps,
        {2 + i: i for i in range(len(held))},
        [pltpu.SemaphoreType.DMA((2, count))],
        count * shape[1] * depth * depth * 8,
    )


def state_grads(flags, queries, out_grad, level_weight, first, count, deps):
    _, length, depth = queries.shape
    levels = level_weight.shape[0] - 1

    def kernel(flag_ref, q_ref, g_ref, w_ref, *outs):
        for i in range(count):
            turned = g_ref[first + i].T.astype(F32)
            weighted = [
                (w_ref[level + 1 : level + 2, :] * flag_ref[level] * turned).astype(BF16)
                for level in range(levels)
            ]
            grads = dot(jnp.concatenate(weighted, axis=0), q_ref[first + i], NN)
            for level in range(levels):
                outs[level][i] = grads[level * depth : (level + 1) * depth]

    return call(
        kernel,
        "state_grads",
        [flags, queries, out_grad, level_weight],
        [SCALARS] + [INSIDE] * 3,
        [jax.ShapeDtypeStruct((count, depth, depth), F32)] * levels,
        [INSIDE] * levels,
        deps,
        flops=count * length * depth * depth * 16,
    )


def local_head(level_weight, queries, key_rows, value_rows, out_grad, held, at, deps):
    heads, length, depth = queries.shape
    tile = min(256, length)

    def kernel(w_ref, q_ref, k_ref, v_ref, g_ref, *rest):
        lq_ref, lk_ref, lv_ref, lw_ref = rest[-4:]
        k_turned = k_ref[at].T
        for i in range(length // tile):
            upto = (i + 1) * tile
            t = pl.ds(i * tile, tile)
            q, g, w = q_ref[at, t, :], g_ref[at, t, :], w_ref[0:1, t]
            raw = dot(k_ref[at, :upto, :], q, NT)
            d_attn = dot(v_ref[at, :upto, :], g, NT)
            rows = lax.broadcasted_iota(jnp.int32, (upto, tile), 0)
            columns = lax.broadcasted_iota(jnp.int32, (upto, tile), 1) + i * tile
            raw = jnp.where(rows <= columns, raw, 0.0)
            d_attn = jnp.where(rows <= columns, d_attn, 0.0)
            lw_ref[0:1, t] = jnp.sum(raw * d_attn, axis=0, keepdims=True)
            attn = (raw * w).astype(BF16)
            d_raw = (d_attn * w).astype(BF16)
            k_part, v_part = dot(d_raw, q, NN), dot(attn, g, NN)
            lk_ref[at, t, :] = k_part[i * tile :]
            lv_ref[at, t, :] = v_part[i * tile :]
            if i:
                lk_ref[at, : i * tile, :] += k_part[: i * tile]
                lv_ref[at, : i * tile, :] += v_part[: i * tile]
            lq_ref[at, :, t] = dot(k_turned[:, :upto], d_raw, NN)

    return call(
        kernel,
        "local",
        [level_weight, queries, key_rows, value_rows, out_grad, *held],
        [INSIDE] * (5 + len(held)),
        [
            pltpu.VMEM((heads, depth, length), F32),
            pltpu.VMEM(queries.shape, F32),
            pltpu.VMEM(queries.shape, F32),
            jax.ShapeDtypeStruct((1, length), F32),
        ],
        [INSIDE] * 4,
        deps,
        {5 + i: i for i in range(len(held))},
        flops=length * length * depth * 12,
    )


def mix(name, flags, arrays, rule, deps):
    def kernel(flag_ref, *refs):
        refs[-1][...] = rule(flag_ref, [ref[...] for ref in refs[:-1]])

    return call(
        kernel,
        name,
        [flags, *arrays],
        [SCALARS] + [INSIDE] * len(arrays),
        [jax.ShapeDtypeStruct(arrays[0].shape, F32)],
        [INSIDE],
        deps,
    )[0]


def keep(flag, array):
    return jnp.where(flag > 0.0, array, 0.0)


def query_side(flags, level_weight, queries, out_grad, query_sum, states, here, first, out, final, deps):
    shape = queries.shape
    _, length, depth = shape
    count = states[0][0].shape[0]
    flat = [part for parts in states for part in parts]
    levels = level_weight.shape[0] - 1
    number = len(here)

    def kernel(flag_ref, w_ref, q_ref, g_ref, sum_ref, *rest):
        if final:
            out_ref, row_ref, staged, sems = rest[-4:]
        else:
            out_ref, row_ref = rest[-2:]
        copies = []
        rows = [None] * number
        for i in range(count):
            parts, at = [], 0
            for j, level in enumerate(here):
                state = rest[at][i]
                if len(states[j]) > 1:
                    state = jnp.where(flag_ref[levels - 2] > 0.0, rest[at + 1][i], state)
                at += len(states[j])
                parts.append(keep(flag_ref[level], state).astype(BF16))
            z_all = dot(jnp.concatenate(parts, axis=0), g_ref[first + i], NT)
            turned = q_ref[first + i].T.astype(F32)
            total = sum_ref[first + i]
            for j, level in enumerate(here):
                z = z_all[j * depth : (j + 1) * depth]
                total = total + w_ref[level + 1 : level + 2, :] * z
                row = jnp.sum(turned * z, axis=0, keepdims=True)
                rows[j] = row if rows[j] is None else rows[j] + row
            if final:
                staged[i] = total.T.astype(BF16)
                copy = pltpu.make_async_copy(staged.at[i], out_ref.at[first + i], sems.at[i])
                copy.start()
                copies.append(copy)
            else:
                out_ref[first + i] = total
        for j in range(number):
            row_ref[j : j + 1, :] = rows[j]
        for copy in copies:
            copy.wait()

    args = [flags, level_weight, queries, out_grad, query_sum, *flat]
    specs = [SCALARS] + [INSIDE] * (len(args) - 1)
    if final:
        aliases = {len(args): 0} if out else {}
        args, specs = args + list(out), specs + [OUTSIDE] * len(out)
        target = jax.ShapeDtypeStruct(shape, BF16)
        scratch = [pltpu.VMEM((count, length, depth), BF16), pltpu.SemaphoreType.DMA((count,))]
    else:
        aliases = {4: 0}
        target = pltpu.VMEM(query_sum.shape, F32)
        scratch = []
    return call(
        kernel,
        "query_side",
        args,
        specs,
        [target, jax.ShapeDtypeStruct((number, length), F32)],
        [OUTSIDE if final else INSIDE, INSIDE],
        deps,
        aliases,
        scratch,
        number * count * length * depth * depth * 8,
    )


def key_side(flags, key_rows, value_rows, key_sum, value_sum, parts, first, out, deps):
    shape = key_rows.shape
    _, length, depth = shape
    count = parts[0].shape[0]
    levels = flags.shape[0]

    def kernel(flag_ref, k_ref, v_ref, ks_ref, vs_ref, *rest):
        k_out, v_out, staged, sems = rest[-4:]
        copies = []
        for i in range(count):
            grad = gathered(flag_ref, [rest[j][i] for j in range(len(parts))]).astype(BF16)
            at = first + i
            staged[0, i] = (ks_ref[at] + dot(v_ref[at], grad, NN)).astype(BF16)
            staged[1, i] = (vs_ref[at] + dot(k_ref[at], grad, NT)).astype(BF16)
            for j, ref in enumerate((k_out, v_out)):
                copy = pltpu.make_async_copy(staged.at[j, i], ref.at[at], sems.at[j, i])
                copy.start()
                copies.append(copy)
        for copy in copies:
            copy.wait()

    args = [flags, key_rows, value_rows, key_sum, value_sum, *parts]
    return call(
        kernel,
        "key_side",
        args + list(out),
        [SCALARS] + [INSIDE] * (len(args) - 1) + [OUTSIDE] * len(out),
        [jax.ShapeDtypeStruct(shape, BF16)] * 2,
        [OUTSIDE] * 2,
        deps,
        {len(args) + i: i for i in range(len(out))},
        [pltpu.VMEM((2, count, length, depth), BF16), pltpu.SemaphoreType.DMA((2, count))],
        count * length * depth * depth * 16,
    )


def bit(n, level):
    return n >> level & 1


def swaps(size):
    levels = size.bit_length() - 1
    top, low = levels - 1, levels - 2
    up = [[(n, n ^ 2**level) for n in range(size)] for level in range(low)]
    across = [(n, n ^ 2**low) for n in range(size)]
    middle = []
    for n in range(size):
        if bit(n, top) != bit(n, low):
            middle.append((n, n ^ 2**top ^ 2**low))
        else:
            middle.append((n, n ^ 1 if low else size - 1 - n))
    return up + [across, middle, across] + up[::-1]


def gathered(flags, terms):
    levels = flags.shape[0]
    top, low = flags[levels - 1], flags[levels - 2]
    total = jnp.where(low > 0.0, keep(1.0 - top, terms[0]), terms[1])
    for term in terms[2:]:
        total = total + term
    return total


def per_device(queries, key_rows, value_rows, level_weight, out_grad):
    size = lax.axis_size("ctx")
    levels = size.bit_length() - 1
    top, low = levels - 1, levels - 2
    heads, length, depth = queries.shape
    position = lax.axis_index("ctx")
    flags = (position // 2 ** jnp.arange(levels, dtype=jnp.int32) % 2).astype(F32)
    counts = PARTS if sum(PARTS) == heads else (heads,)
    parts = range(len(counts))
    firsts = [sum(counts[:part]) for part in parts]
    steps = swaps(size)

    def inside(array):
        return pltpu.with_memory_space_constraint(array, pltpu.VMEM)

    def outside(array):
        return pltpu.with_memory_space_constraint(array, pltpu.HBM)

    q_in, g_in = inside(queries), inside(out_grad)
    k_out, v_out = outside(key_rows), outside(value_rows)
    w_in = level_weight
    kv, got, grads = [], [[] for _ in parts], [None for _ in parts]
    ups = [None for _ in parts]
    dep = []
    for part in parts:
        *kv, state = load_states(k_out, v_out, kv, firsts[part], counts[part], dep)
        ups[part] = [state]
        dep = [state]
        if low:
            got[part].append(lax.ppermute(state, "ctx", steps[0]))
    k_in, v_in = kv

    held, rows, todo = [], [], list(range(heads))
    early, late = list(parts), list(parts)
    early_rows, late_rows = [], []
    query_out = []

    def make_grads(part, dep):
        grads[part] = state_grads(flags, q_in, g_in, w_in, firsts[part], counts[part], dep)
        return [grads[part][top]]

    def local(dep):
        nonlocal held
        if todo:
            *held, row = local_head(w_in, q_in, k_in, v_in, g_in, held, todo.pop(0), dep)
            rows.append(row)
            dep = [row]
        return dep

    def query(part, here, states, final, dep):
        out, row = query_side(
            flags, w_in, q_in, g_in, held[0], states, here, firsts[part], query_out, final, dep
        )
        if final:
            query_out[:] = [out]
        else:
            held[0] = out
        return row

    def early_query(dep):
        part = early.pop(0)
        row = query(part, list(range(top)), [[got[part][level]] for level in range(top)], False, dep)
        early_rows.append(row)
        return [row]

    def late_query(dep):
        part = late.pop(0)
        row = query(part, [top], [[got[part][top], got[part][top + 1]]], True, dep)
        late_rows.append(row)
        return [row]

    def advance(step, part, dep):
        have, grad = got[part], grads[part]
        if step < low:
            terms = ups[part] + have

            def rule(flag, terms):
                return sum(terms[1:], terms[0])

        elif step == low:
            terms = ups[part] + have + [grad[top]]

            def rule(flag, terms):
                return jnp.where(flag[low] > 0.0, terms[-1], sum(terms[1:-1], terms[0]))

        elif step == low + 1:
            terms = ups[part] + have[:low] + [grad[top], have[low]]

            def rule(flag, terms):
                up = sum(terms[1:-2], terms[0])
                return jnp.where(flag[top] > 0.0, terms[-2], up) + terms[-1]

        elif step == low + 2:
            terms = [grad[low], have[low + 1]]

            def rule(flag, terms):
                other = keep(1.0 - flag[low] * flag[top], terms[1])
                return keep(flag[low], terms[0]) + other

        else:
            level = 2 * low + 2 - step
            terms = [grad[level], *have[low + 1 :]]

            def rule(flag, terms):
                return terms[0] + gathered(flag, terms[1:])

        sent = mix("mix", flags, terms, rule, dep)
        have.append(lax.ppermute(sent, "ctx", steps[step]))
        return [sent]

    for part in parts:
        dep = make_grads(part, dep)
    fill = list(FILL)
    for step in range(1 if low else 0, len(steps)):
        for part in parts:
            for _ in range(fill.pop(0) if fill else 0):
                dep = local(dep)
            dep = advance(step, part, dep)
        if step == low + 2:
            for _ in todo[:]:
                dep = local(dep)
            for _ in parts:
                dep = early_query(dep)
        if step == low + 3:
            for _ in parts:
                dep = late_query(dep)
    while late:
        dep = late_query(dep)

    weight_grad = jnp.concatenate([sum(rows), sum(early_rows), sum(late_rows)], axis=0)
    ways = lax.axis_size("head")
    others = [
        lax.ppermute(weight_grad, "head", [(n, (n + shift) % ways) for n in range(ways)])
        for shift in range(1, ways)
    ]
    key_out = []
    for part in parts:
        key_out = key_side(
            flags, k_in, v_in, held[1], held[2], got[part][low + 1 :], firsts[part], key_out, dep
        )
        dep = []
    for other in others:
        weight_grad = weight_grad + other
    return query_out[0], key_out[0], key_out[1], weight_grad


def solution(mesh):
    placed = (
        P("head", "ctx", None),
        P("head", "ctx", None),
        P("head", "ctx", None),
        P(None, "ctx"),
        P("head", "ctx", None),
    )
    return jax.shard_map(
        per_device,
        mesh=mesh,
        in_specs=placed,
        out_specs=(
            P("head", "ctx", None),
            P("head", "ctx", None),
            P("head", "ctx", None),
            P(None, "ctx"),
        ),
        check_vma=False,
    )
```

```python
import jax
import jax.numpy as jnp
from jax import lax
from jax.experimental import pallas as pl
from jax.experimental.pallas import tpu as pltpu
from jax.sharding import PartitionSpec as P

F32, BF16 = jnp.float32, jnp.bfloat16
NN = (((1,), (0,)), ((), ()))
NT = (((1,), (1,)), ((), ()))
TN = (((0,), (0,)), ((), ()))
VMEM_BYTES = 16 * 2**20
PARTS = (4, 4)
FILL = (0, 1, 1, 1, 2, 1, 2, 0)

INSIDE = pl.BlockSpec(memory_space=pltpu.VMEM)
OUTSIDE = pl.BlockSpec(memory_space=pltpu.HBM)
ANYWHERE = pl.BlockSpec(memory_space=pl.ANY)


def dot(a, b, dims):
    return lax.dot_general(a, b, dims, preferred_element_type=F32)


def block_bits(levels):
    position = lax.axis_index("ctx")
    return [(position >> level & 1) == 1 for level in range(levels)]


def inside(array):
    return pltpu.with_memory_space_constraint(array, pltpu.VMEM)


def outside(array):
    return pltpu.with_memory_space_constraint(array, pltpu.HBM)


def call(kernel, name, args, specs, outs, out_specs, deps=(), aliases=None, scratch=()):
    deps = list(deps)
    count = len(args)
    args = [
        inside(arg) if spec is INSIDE else outside(arg) if spec is OUTSIDE else arg
        for arg, spec in zip(args, specs, strict=True)
    ]

    def body(*refs):
        kernel(*refs[:count], *refs[count + len(deps) :])

    return pl.pallas_call(
        body,
        in_specs=list(specs) + [ANYWHERE] * len(deps),
        out_specs=list(out_specs),
        out_shape=list(outs),
        scratch_shapes=list(scratch),
        input_output_aliases=aliases or {},
        compiler_params=pltpu.CompilerParams(vmem_limit_bytes=VMEM_BYTES),
        cost_estimate=pl.CostEstimate(flops=1, bytes_accessed=1, transcendentals=0),
        name=name,
    )(*args, *deps)


def load_states(pairs, held, first, count, deps):
    shape = pairs[0].shape
    depth = shape[2]
    number = len(pairs)

    def kernel(*refs):
        sems = refs[-1]
        state = refs[-2]
        inner = refs[-2 - number : -2]
        halves = [(0, count // 2), (count // 2, count)] if count > 1 else [(0, 1)]
        copies = []
        for half, (start, stop) in enumerate(halves):
            at = pl.ds(first + start, stop - start)
            for j in range(2):
                copies.append(
                    pltpu.make_async_copy(refs[j].at[at], inner[j].at[at], sems.at[j, half])
                )
        for j in range(2, number):
            copies.append(pltpu.make_async_copy(refs[j], inner[j], sems.at[j, 0]))
        for copy in copies:
            copy.start()
        for half, (start, stop) in enumerate(halves):
            copies[2 * half].wait()
            copies[2 * half + 1].wait()
            for i in range(start, stop):
                state[i] = dot(inner[0][first + i], inner[1][first + i], TN)
        for copy in copies[2 * len(halves) :]:
            copy.wait()

    kind = pltpu.VMEM(shape, BF16)
    return call(
        kernel,
        "load_states",
        [*pairs, *held],
        [OUTSIDE] * number + [INSIDE] * len(held),
        [kind] * number + [jax.ShapeDtypeStruct((count, depth, depth), F32)],
        [INSIDE] * (number + 1),
        deps,
        {number + i: i for i in range(len(held))},
        [pltpu.SemaphoreType.DMA((number, 2))],
    )


def state_grads(queries, out_grad, level_weight, first, count, deps):
    _, length, depth = queries.shape
    levels = level_weight.shape[0] - 1

    def kernel(q_ref, g_ref, w_ref, *outs):
        bits = block_bits(levels)
        for i in range(count):
            turned = g_ref[first + i].T.astype(F32)
            weighted = [
                (keep(bits[level], w_ref[level + 1 : level + 2, :]) * turned).astype(BF16)
                for level in range(levels)
            ]
            grads = dot(jnp.concatenate(weighted, axis=0), q_ref[first + i], NN)
            for level in range(levels):
                outs[level][i] = grads[level * depth : (level + 1) * depth]

    return call(
        kernel,
        "state_grads",
        [queries, out_grad, level_weight],
        [INSIDE] * 3,
        [jax.ShapeDtypeStruct((count, depth, depth), F32)] * levels,
        [INSIDE] * levels,
        deps,
    )


def local_head(level_weight, queries, key_rows, value_rows, out_grad, held, at, deps):
    heads, length, depth = queries.shape
    tile = min(256, length)

    def kernel(w_ref, q_ref, k_ref, v_ref, g_ref, *rest):
        lq_ref, lk_ref, lv_ref, lw_ref = rest[-4:]
        k_turned = k_ref[at].T
        for i in range(length // tile):
            upto = (i + 1) * tile
            t = pl.ds(i * tile, tile)
            q, g, w = q_ref[at, t, :], g_ref[at, t, :], w_ref[0:1, t]
            raw = dot(k_ref[at, :upto, :], q, NT)
            d_attn = dot(v_ref[at, :upto, :], g, NT)
            rows = lax.broadcasted_iota(jnp.int32, (upto, tile), 0)
            columns = lax.broadcasted_iota(jnp.int32, (upto, tile), 1) + i * tile
            raw = jnp.where(rows <= columns, raw, 0.0)
            d_attn = jnp.where(rows <= columns, d_attn, 0.0)
            lw_ref[0:1, t] = jnp.sum(raw * d_attn, axis=0, keepdims=True)
            attn = (raw * w).astype(BF16)
            d_raw = (d_attn * w).astype(BF16)
            k_part, v_part = dot(d_raw, q, NN), dot(attn, g, NN)
            lk_ref[at, t, :] = k_part[i * tile :]
            lv_ref[at, t, :] = v_part[i * tile :]
            if i:
                lk_ref[at, : i * tile, :] += k_part[: i * tile]
                lv_ref[at, : i * tile, :] += v_part[: i * tile]
            lq_ref[at, :, t] = dot(k_turned[:, :upto], d_raw, NN)

    return call(
        kernel,
        "local",
        [level_weight, queries, key_rows, value_rows, out_grad, *held],
        [INSIDE] * (5 + len(held)),
        [
            pltpu.VMEM((heads, depth, length), F32),
            pltpu.VMEM(queries.shape, F32),
            pltpu.VMEM(queries.shape, F32),
            jax.ShapeDtypeStruct((1, length), F32),
        ],
        [INSIDE] * 4,
        deps,
        {5 + i: i for i in range(len(held))},
    )


def mix(levels, arrays, rule, deps):
    def kernel(*refs):
        refs[-1][...] = rule(block_bits(levels), [ref[...] for ref in refs[:-1]])

    return call(
        kernel,
        "mix",
        arrays,
        [INSIDE] * len(arrays),
        [jax.ShapeDtypeStruct(arrays[0].shape, F32)],
        [INSIDE],
        deps,
    )[0]


def keep(flag, array):
    return jnp.where(flag, array, 0.0)


def query_side(level_weight, queries, out_grad, query_sum, states, rows, first, out, deps):
    shape = queries.shape
    _, length, depth = shape
    count = states[0].shape[0]
    levels = len(states) - 1
    single, whole = rows

    def kernel(w_ref, q_ref, g_ref, sum_ref, *rest):
        state_refs = rest[: levels + 1]
        singles = rest[levels + 1 : levels + 1 + len(single)]
        wholes = rest[levels + 1 + len(single) : levels + 1 + len(single) + len(whole)]
        out_ref, row_ref, staged, sems = rest[-4:]
        bits = block_bits(levels)
        copies = []
        totals = [None] * levels

        def product(i):
            parts = [state_refs[level][i] for level in range(levels)]
            parts[-1] = jnp.where(bits[levels - 2], state_refs[levels][i], parts[-1])
            parts = [keep(bit_here, part).astype(BF16) for bit_here, part in zip(bits, parts, strict=True)]
            return dot(jnp.concatenate(parts, axis=0), g_ref[first + i], NT)

        later = product(0)
        for i in range(count):
            z_all = later
            if i + 1 < count:
                later = product(i + 1)
            turned = q_ref[first + i].T.astype(F32)
            total = sum_ref[first + i]
            for level in range(levels):
                z = z_all[level * depth : (level + 1) * depth]
                total = total + w_ref[level + 1 : level + 2, :] * z
                row = jnp.sum(turned * z, axis=0, keepdims=True)
                totals[level] = row if totals[level] is None else totals[level] + row
            staged[i] = total.T.astype(BF16)
            copy = pltpu.make_async_copy(staged.at[i], out_ref.at[first + i], sems.at[i])
            copy.start()
            copies.append(copy)
        own = None
        for ref in singles:
            own = ref[...] if own is None else own + ref[...]
        for ref in wholes:
            own = ref[0:1, :] if own is None else own + ref[0:1, :]
            for level in range(levels):
                totals[level] += ref[level + 1 : level + 2, :]
        row_ref[0:1, :] = own
        for level in range(levels):
            row_ref[level + 1 : level + 2, :] = totals[level]
        for copy in copies:
            copy.wait()

    args = [level_weight, queries, out_grad, query_sum, *states, *single, *whole]
    return call(
        kernel,
        "query_side",
        args + list(out),
        [INSIDE] * len(args) + [OUTSIDE] * len(out),
        [jax.ShapeDtypeStruct(shape, BF16), jax.ShapeDtypeStruct((levels + 1, length), F32)],
        [OUTSIDE, INSIDE],
        deps,
        {len(args): 0} if out else {},
        [pltpu.VMEM((count, length, depth), BF16), pltpu.SemaphoreType.DMA((count,))],
    )


def key_side(key_rows, value_rows, key_sum, value_sum, parts, levels, rows, first, out, deps):
    shape = key_rows.shape
    _, length, depth = shape
    count = parts[0].shape[0]
    summed = [jax.ShapeDtypeStruct(rows[0].shape, F32)] if rows else []

    def kernel(k_ref, v_ref, ks_ref, vs_ref, *rest):
        k_out, v_out = rest[len(parts) + len(rows) + len(out) :][:2]
        staged, sems = rest[-2 - 2 * len(summed) :][:2]
        bits = block_bits(levels)
        copies = []
        if rows:
            total = rest[len(parts)][...]
            for ref in rest[len(parts) + 1 : len(parts) + len(rows)]:
                total = total + ref[...]
            rest[-2][...] = total
            copies.append(pltpu.make_async_copy(rest[-2], rest[-5], rest[-1]))
            copies[0].start()

        def products(i):
            grad = gathered(bits, [rest[j][i] for j in range(len(parts))]).astype(BF16)
            return dot(v_ref[first + i], grad, NN), dot(k_ref[first + i], grad, NT)

        later = products(0)
        for i in range(count):
            added = later
            if i + 1 < count:
                later = products(i + 1)
            at = first + i
            for j, (ref, sum_ref) in enumerate(((k_out, ks_ref), (v_out, vs_ref))):
                staged[j, i] = (sum_ref[at] + added[j]).astype(BF16)
                copy = pltpu.make_async_copy(staged.at[j, i], ref.at[at], sems.at[j, i])
                copy.start()
                copies.append(copy)
        for copy in copies:
            copy.wait()

    args = [key_rows, value_rows, key_sum, value_sum, *parts, *rows]
    return call(
        kernel,
        "key_side",
        args + list(out),
        [INSIDE] * len(args) + [OUTSIDE] * len(out),
        [jax.ShapeDtypeStruct(shape, BF16)] * 2 + summed,
        [OUTSIDE] * (2 + len(summed)),
        deps,
        {len(args) + i: i for i in range(len(out))},
        [pltpu.VMEM((2, count, length, depth), BF16), pltpu.SemaphoreType.DMA((2, count))]
        + ([pltpu.VMEM(rows[0].shape, F32), pltpu.SemaphoreType.DMA] if rows else []),
    )


def bit(n, level):
    return n >> level & 1


def swaps(size):
    levels = size.bit_length() - 1
    top, low = levels - 1, levels - 2
    up = [[(n, n ^ 2**level) for n in range(size)] for level in range(low)]
    across = [(n, n ^ 2**low) for n in range(size)]
    middle = []
    for n in range(size):
        if bit(n, top) != bit(n, low):
            middle.append((n, n ^ 2**top ^ 2**low))
        else:
            middle.append((n, n ^ 1 if low else size - 1 - n))
    return up + [across, middle, across] + up[::-1]


def gathered(bits, terms):
    top, low = bits[-1], bits[-2]
    total = jnp.where(low, keep(~top, terms[0]), terms[1])
    for term in terms[2:]:
        total = total + term
    return total


def per_device(queries, key_rows, value_rows, level_weight, out_grad):
    size = lax.axis_size("ctx")
    levels = size.bit_length() - 1
    top, low = levels - 1, levels - 2
    heads = queries.shape[0]
    counts = PARTS if sum(PARTS) == heads else (heads,)
    parts = range(len(counts))
    firsts = [sum(counts[:part]) for part in parts]
    steps = swaps(size)
    w_in = level_weight
    got, grads, ups = [[] for _ in parts], [None for _ in parts], [None for _ in parts]
    inner, dep = [], []
    for part in parts:
        more = part == parts[-1]
        pairs = [key_rows, value_rows] + ([queries, out_grad] if more else [])
        *inner, state = load_states(pairs, inner, firsts[part], counts[part], dep)
        ups[part] = [state]
        dep = [state]
        if low:
            got[part].append(lax.ppermute(state, "ctx", steps[0]))
    k_in, v_in, q_in, g_in = inner

    held, rows, todo = [], [], list(range(heads))

    def local(dep):
        nonlocal held
        if todo:
            *held, row = local_head(w_in, q_in, k_in, v_in, g_in, held, todo.pop(0), dep)
            rows.append(row)
            dep = [row]
        return dep

    def advance(step, part, dep):
        have, grad = got[part], grads[part]
        if step < low:
            terms = ups[part] + have

            def rule(bits, terms):
                return sum(terms[1:], terms[0])

        elif step == low:
            terms = ups[part] + have + [grad[top]]

            def rule(bits, terms):
                return jnp.where(bits[low], terms[-1], sum(terms[1:-1], terms[0]))

        elif step == low + 1:
            terms = ups[part] + have[:low] + [grad[top], have[low]]

            def rule(bits, terms):
                up = sum(terms[1:-2], terms[0])
                return jnp.where(bits[top], terms[-2], up) + terms[-1]

        elif step == low + 2:
            terms = [grad[low], have[low + 1]]

            def rule(bits, terms):
                other = jnp.where(bits[low], keep(~bits[top], terms[1]), terms[1])
                return keep(bits[low], terms[0]) + other

        else:
            terms = [grad[2 * low + 2 - step], *have[low + 1 :]]

            def rule(bits, terms):
                return terms[0] + gathered(bits, terms[1:])

        sent = mix(levels, terms, rule, dep)
        have.append(lax.ppermute(sent, "ctx", steps[step]))
        return [sent]

    for part in parts:
        grads[part] = state_grads(q_in, g_in, w_in, firsts[part], counts[part], dep)
        dep = [grads[part][top]]

    query_out, weight_rows, asked = [], [], list(parts)

    def query(dep):
        part = asked.pop(0)
        grad, row = query_side(
            w_in,
            q_in,
            g_in,
            held[0],
            got[part][: levels + 1],
            ([] if weight_rows else rows, weight_rows),
            firsts[part],
            query_out,
            dep,
        )
        query_out[:], weight_rows[:] = [grad], [row]
        return [row]

    fill = list(FILL)
    for step in range(1 if low else 0, len(steps)):
        for part in parts:
            if step == low + 3 and part:
                dep = query(dep)
            for _ in range(fill.pop(0) if fill else 0):
                dep = local(dep)
            dep = advance(step, part, dep)
    while todo:
        dep = local(dep)
    while asked:
        dep = query(dep)
    ways = lax.axis_size("head")
    weight_rows += [
        lax.ppermute(weight_rows[0], "head", [(n, (n + shift) % ways) for n in range(ways)])
        for shift in range(1, ways)
    ]
    key_out, weight_grad = [], None
    for part in parts:
        *key_out, weight_grad = [
            *key_side(
                k_in,
                v_in,
                held[1],
                held[2],
                got[part][low + 1 :],
                levels,
                weight_rows if part == parts[-1] else [],
                firsts[part],
                key_out,
                dep,
            ),
            *([] if part == parts[-1] else [None]),
        ]
        dep = []
    return query_out[0], key_out[0], key_out[1], weight_grad


def solution(mesh):
    placed = (
        P("head", "ctx", None),
        P("head", "ctx", None),
        P("head", "ctx", None),
        P(None, "ctx"),
        P("head", "ctx", None),
    )
    return jax.shard_map(
        per_device,
        mesh=mesh,
        in_specs=placed,
        out_specs=(
            P("head", "ctx", None),
            P("head", "ctx", None),
            P("head", "ctx", None),
            P(None, "ctx"),
        ),
        check_vma=False,
    )
```

```python
import jax
import jax.numpy as jnp
from jax import lax
from jax.experimental import pallas as pl
from jax.experimental.pallas import tpu as pltpu
from jax.sharding import PartitionSpec as P

F32, BF16 = jnp.float32, jnp.bfloat16
NN = (((1,), (0,)), ((), ()))
NT = (((1,), (1,)), ((), ()))
TN = (((0,), (0,)), ((), ()))
VMEM_BYTES = 16 * 2**20
PARTS = (4, 4)
FILL = (1, 2, 1, 1, 1, 1, 1, 0)

INSIDE = pl.BlockSpec(memory_space=pltpu.VMEM)
OUTSIDE = pl.BlockSpec(memory_space=pltpu.HBM)
ANYWHERE = pl.BlockSpec(memory_space=pl.ANY)


def dot(a, b, dims):
    return lax.dot_general(a, b, dims, preferred_element_type=F32)


def block_bits(levels):
    position = lax.axis_index("ctx")
    return [(position >> level & 1) == 1 for level in range(levels)]


def inside(array):
    return pltpu.with_memory_space_constraint(array, pltpu.VMEM)


def outside(array):
    return pltpu.with_memory_space_constraint(array, pltpu.HBM)


def call(kernel, name, args, specs, outs, out_specs, deps=(), aliases=None, scratch=()):
    deps = list(deps)
    count = len(args)
    args = [
        inside(arg) if spec is INSIDE else outside(arg) if spec is OUTSIDE else arg
        for arg, spec in zip(args, specs, strict=True)
    ]

    def body(*refs):
        kernel(*refs[:count], *refs[count + len(deps) :])

    return pl.pallas_call(
        body,
        in_specs=list(specs) + [ANYWHERE] * len(deps),
        out_specs=list(out_specs),
        out_shape=list(outs),
        scratch_shapes=list(scratch),
        input_output_aliases=aliases or {},
        compiler_params=pltpu.CompilerParams(vmem_limit_bytes=VMEM_BYTES),
        cost_estimate=pl.CostEstimate(flops=1, bytes_accessed=1, transcendentals=0),
        name=name,
    )(*args, *deps)


def load_states(pairs, held, first, count, deps):
    shape = pairs[0].shape
    depth = shape[2]
    number = len(pairs)

    def kernel(*refs):
        sems = refs[-1]
        state = refs[-2]
        inner = refs[-2 - number : -2]
        halves = [(0, count // 2), (count // 2, count)] if count > 1 else [(0, 1)]
        copies = []
        for half, (start, stop) in enumerate(halves):
            at = pl.ds(first + start, stop - start)
            for j in range(2):
                copies.append(
                    pltpu.make_async_copy(refs[j].at[at], inner[j].at[at], sems.at[j, half])
                )
        for j in range(2, number):
            copies.append(pltpu.make_async_copy(refs[j], inner[j], sems.at[j, 0]))
        for copy in copies:
            copy.start()
        for half, (start, stop) in enumerate(halves):
            copies[2 * half].wait()
            copies[2 * half + 1].wait()
            for i in range(start, stop):
                state[i] = dot(inner[0][first + i], inner[1][first + i], TN)
        for copy in copies[2 * len(halves) :]:
            copy.wait()

    kind = pltpu.VMEM(shape, BF16)
    return call(
        kernel,
        "load_states",
        [*pairs, *held],
        [OUTSIDE] * number + [INSIDE] * len(held),
        [kind] * number + [jax.ShapeDtypeStruct((count, depth, depth), F32)],
        [INSIDE] * (number + 1),
        deps,
        {number + i: i for i in range(len(held))},
        [pltpu.SemaphoreType.DMA((number, 2))],
    )


def state_grads(queries, out_grad, level_weight, first, count, deps):
    _, length, depth = queries.shape
    levels = level_weight.shape[0] - 1

    def kernel(q_ref, g_ref, w_ref, *outs):
        bits = block_bits(levels)
        for i in range(count):
            turned = g_ref[first + i].T.astype(F32)
            weighted = [
                (keep(bits[level], w_ref[level + 1 : level + 2, :]) * turned).astype(BF16)
                for level in range(levels)
            ]
            grads = dot(jnp.concatenate(weighted, axis=0), q_ref[first + i], NN)
            for level in range(levels):
                outs[level][i] = grads[level * depth : (level + 1) * depth]

    return call(
        kernel,
        "state_grads",
        [queries, out_grad, level_weight],
        [INSIDE] * 3,
        [jax.ShapeDtypeStruct((count, depth, depth), F32)] * levels,
        [INSIDE] * levels,
        deps,
    )


def local_head(level_weight, queries, key_rows, value_rows, out_grad, held, at, deps):
    heads, length, depth = queries.shape
    tile = min(256, length)

    def kernel(w_ref, q_ref, k_ref, v_ref, g_ref, *rest):
        lq_ref, lk_ref, lv_ref, lw_ref = rest[-4:]
        k_turned = k_ref[at].T
        tiles = length // tile

        def products(i):
            upto = (i + 1) * tile
            t = pl.ds(i * tile, tile)
            raw = dot(k_ref[at, :upto, :], q_ref[at, t, :], NT)
            return raw, dot(v_ref[at, :upto, :], g_ref[at, t, :], NT)

        later = products(0)
        for i in range(tiles):
            raw, d_attn = later
            if i + 1 < tiles:
                later = products(i + 1)
            upto = (i + 1) * tile
            t = pl.ds(i * tile, tile)
            w = w_ref[0:1, t]
            rows = lax.broadcasted_iota(jnp.int32, (upto, tile), 0)
            columns = lax.broadcasted_iota(jnp.int32, (upto, tile), 1) + i * tile
            raw = jnp.where(rows <= columns, raw, 0.0)
            d_attn = jnp.where(rows <= columns, d_attn, 0.0)
            lw_ref[0:1, t] = jnp.sum(raw * d_attn, axis=0, keepdims=True)
            attn = (raw * w).astype(BF16)
            d_raw = (d_attn * w).astype(BF16)
            k_part = dot(d_raw, q_ref[at, t, :], NN)
            v_part = dot(attn, g_ref[at, t, :], NN)
            lk_ref[at, t, :] = k_part[i * tile :]
            lv_ref[at, t, :] = v_part[i * tile :]
            if i:
                lk_ref[at, : i * tile, :] += k_part[: i * tile]
                lv_ref[at, : i * tile, :] += v_part[: i * tile]
            lq_ref[at, :, t] = dot(k_turned[:, :upto], d_raw, NN)

    return call(
        kernel,
        "local",
        [level_weight, queries, key_rows, value_rows, out_grad, *held],
        [INSIDE] * (5 + len(held)),
        [
            pltpu.VMEM((heads, depth, length), F32),
            pltpu.VMEM(queries.shape, F32),
            pltpu.VMEM(queries.shape, F32),
            jax.ShapeDtypeStruct((1, length), F32),
        ],
        [INSIDE] * 4,
        deps,
        {5 + i: i for i in range(len(held))},
    )


def mix(levels, arrays, rule, deps):
    def kernel(*refs):
        refs[-1][...] = rule(block_bits(levels), [ref[...] for ref in refs[:-1]])

    return call(
        kernel,
        "mix",
        arrays,
        [INSIDE] * len(arrays),
        [jax.ShapeDtypeStruct(arrays[0].shape, F32)],
        [INSIDE],
        deps,
    )[0]


def keep(flag, array):
    return jnp.where(flag, array, 0.0)


def query_side(level_weight, queries, out_grad, query_sum, states, rows, first, out, deps):
    shape = queries.shape
    _, length, depth = shape
    count = states[0].shape[0]
    levels = len(states) - 1
    single, whole = rows

    def kernel(w_ref, q_ref, g_ref, sum_ref, *rest):
        state_refs = rest[: levels + 1]
        singles = rest[levels + 1 : levels + 1 + len(single)]
        wholes = rest[levels + 1 + len(single) : levels + 1 + len(single) + len(whole)]
        out_ref, row_ref = rest[-2:]
        bits = block_bits(levels)
        totals = [None] * levels

        def product(i):
            parts = [state_refs[level][i] for level in range(levels)]
            parts[-1] = jnp.where(bits[levels - 2], state_refs[levels][i], parts[-1])
            parts = [keep(bit_here, part).astype(BF16) for bit_here, part in zip(bits, parts, strict=True)]
            return dot(jnp.concatenate(parts, axis=0), g_ref[first + i], NT)

        later = product(0)
        for i in range(count):
            z_all = later
            if i + 1 < count:
                later = product(i + 1)
            turned = q_ref[first + i].T.astype(F32)
            total = sum_ref[first + i]
            for level in range(levels):
                z = z_all[level * depth : (level + 1) * depth]
                total = total + w_ref[level + 1 : level + 2, :] * z
                row = jnp.sum(turned * z, axis=0, keepdims=True)
                totals[level] = row if totals[level] is None else totals[level] + row
            out_ref[first + i] = total.T.astype(BF16)
        own = None
        for ref in singles:
            own = ref[...] if own is None else own + ref[...]
        for ref in wholes:
            own = ref[0:1, :] if own is None else own + ref[0:1, :]
            for level in range(levels):
                totals[level] += ref[level + 1 : level + 2, :]
        row_ref[0:1, :] = own
        for level in range(levels):
            row_ref[level + 1 : level + 2, :] = totals[level]

    args = [level_weight, queries, out_grad, query_sum, *states, *single, *whole]
    return call(
        kernel,
        "query_side",
        args + list(out),
        [INSIDE] * (len(args) + len(out)),
        [pltpu.VMEM(shape, BF16), jax.ShapeDtypeStruct((levels + 1, length), F32)],
        [INSIDE] * 2,
        deps,
        {len(args): 0} if out else {},
    )


def key_side(key_rows, value_rows, key_sum, value_sum, parts, levels, rows, first, out, deps):
    shape = key_rows.shape
    _, length, depth = shape
    count = parts[0].shape[0]
    summed = [jax.ShapeDtypeStruct(rows[0].shape, F32)] if rows else []

    def kernel(k_ref, v_ref, ks_ref, vs_ref, *rest):
        k_out, v_out = rest[len(parts) + len(rows) + len(out) :][:2]
        staged, sems = rest[-2 - 2 * len(summed) :][:2]
        bits = block_bits(levels)
        copies = []
        if rows:
            total = rest[len(parts)][...]
            for ref in rest[len(parts) + 1 : len(parts) + len(rows)]:
                total = total + ref[...]
            rest[-2][...] = total
            copies.append(pltpu.make_async_copy(rest[-2], rest[-5], rest[-1]))
            copies[0].start()

        def products(i):
            grad = gathered(bits, [rest[j][i] for j in range(len(parts))]).astype(BF16)
            return dot(v_ref[first + i], grad, NN), dot(k_ref[first + i], grad, NT)

        later = products(0)
        for i in range(count):
            added = later
            if i + 1 < count:
                later = products(i + 1)
            at = first + i
            for j, (ref, sum_ref) in enumerate(((k_out, ks_ref), (v_out, vs_ref))):
                staged[j, i] = (sum_ref[at] + added[j]).astype(BF16)
                copy = pltpu.make_async_copy(staged.at[j, i], ref.at[at], sems.at[j, i])
                copy.start()
                copies.append(copy)
        for copy in copies:
            copy.wait()

    args = [key_rows, value_rows, key_sum, value_sum, *parts, *rows]
    return call(
        kernel,
        "key_side",
        args + list(out),
        [INSIDE] * len(args) + [OUTSIDE] * len(out),
        [jax.ShapeDtypeStruct(shape, BF16)] * 2 + summed,
        [OUTSIDE] * (2 + len(summed)),
        deps,
        {len(args) + i: i for i in range(len(out))},
        [pltpu.VMEM((2, count, length, depth), BF16), pltpu.SemaphoreType.DMA((2, count))]
        + ([pltpu.VMEM(rows[0].shape, F32), pltpu.SemaphoreType.DMA] if rows else []),
    )


def bit(n, level):
    return n >> level & 1


def swaps(size):
    levels = size.bit_length() - 1
    top, low = levels - 1, levels - 2
    up = [[(n, n ^ 2**level) for n in range(size)] for level in range(low)]
    across = [(n, n ^ 2**low) for n in range(size)]
    middle = []
    for n in range(size):
        if bit(n, top) != bit(n, low):
            middle.append((n, n ^ 2**top ^ 2**low))
        else:
            middle.append((n, n ^ 1 if low else size - 1 - n))
    return up + [across, middle, across] + up[::-1]


def gathered(bits, terms):
    top, low = bits[-1], bits[-2]
    total = jnp.where(low, keep(~top, terms[0]), terms[1])
    for term in terms[2:]:
        total = total + term
    return total


def per_device(queries, key_rows, value_rows, level_weight, out_grad):
    size = lax.axis_size("ctx")
    levels = size.bit_length() - 1
    top, low = levels - 1, levels - 2
    heads = queries.shape[0]
    counts = PARTS if sum(PARTS) == heads else (heads,)
    parts = range(len(counts))
    firsts = [sum(counts[:part]) for part in parts]
    steps = swaps(size)
    w_in = level_weight
    got, grads, ups = [[] for _ in parts], [None for _ in parts], [None for _ in parts]
    inner, dep = [], []
    for part in parts:
        more = part == parts[-1]
        pairs = [key_rows, value_rows] + ([queries, out_grad] if more else [])
        *inner, state = load_states(pairs, inner, firsts[part], counts[part], dep)
        ups[part] = [state]
        dep = [state]
        if low:
            got[part].append(lax.ppermute(state, "ctx", steps[0]))
    k_in, v_in, q_in, g_in = inner

    held, rows, todo = [], [], list(range(heads))

    def local(dep):
        nonlocal held
        if todo:
            *held, row = local_head(w_in, q_in, k_in, v_in, g_in, held, todo.pop(0), dep)
            rows.append(row)
            dep = [row]
        return dep

    def advance(step, part, dep):
        have, grad = got[part], grads[part]
        if step < low:
            terms = ups[part] + have

            def rule(bits, terms):
                return sum(terms[1:], terms[0])

        elif step == low:
            terms = ups[part] + have + [grad[top]]

            def rule(bits, terms):
                return jnp.where(bits[low], terms[-1], sum(terms[1:-1], terms[0]))

        elif step == low + 1:
            terms = ups[part] + have[:low] + [grad[top], have[low]]

            def rule(bits, terms):
                up = sum(terms[1:-2], terms[0])
                return jnp.where(bits[top], terms[-2], up) + terms[-1]

        elif step == low + 2:
            terms = [grad[low], have[low + 1]]

            def rule(bits, terms):
                other = jnp.where(bits[low], keep(~bits[top], terms[1]), terms[1])
                return keep(bits[low], terms[0]) + other

        else:
            terms = [grad[2 * low + 2 - step], *have[low + 1 :]]

            def rule(bits, terms):
                return terms[0] + gathered(bits, terms[1:])

        sent = mix(levels, terms, rule, dep)
        have.append(lax.ppermute(sent, "ctx", steps[step]))
        return [sent]

    for part in parts:
        grads[part] = state_grads(q_in, g_in, w_in, firsts[part], counts[part], dep)
        dep = [grads[part][top]]

    query_out, weight_rows, asked = [], [], list(parts)

    def query(dep):
        part = asked.pop(0)
        grad, row = query_side(
            w_in,
            q_in,
            g_in,
            held[0],
            got[part][: levels + 1],
            ([] if weight_rows else rows, weight_rows),
            firsts[part],
            query_out,
            dep,
        )
        query_out[:], weight_rows[:] = [grad], [row]
        return [row]

    fill = list(FILL)
    for step in range(1 if low else 0, len(steps)):
        for part in parts:
            if step == low + 3 and part:
                dep = query(dep)
            for _ in range(fill.pop(0) if fill else 0):
                dep = local(dep)
            dep = advance(step, part, dep)
    while todo:
        dep = local(dep)
    while asked:
        dep = query(dep)
    ways = lax.axis_size("head")
    weight_rows += [
        lax.ppermute(weight_rows[0], "head", [(n, (n + shift) % ways) for n in range(ways)])
        for shift in range(1, ways)
    ]
    key_out, weight_grad = [], None
    for part in parts:
        *key_out, weight_grad = [
            *key_side(
                k_in,
                v_in,
                held[1],
                held[2],
                got[part][low + 1 :],
                levels,
                weight_rows if part == parts[-1] else [],
                firsts[part],
                key_out,
                dep,
            ),
            *([] if part == parts[-1] else [None]),
        ]
        dep = []
    return query_out[0], key_out[0], key_out[1], weight_grad


def solution(mesh):
    placed = (
        P("head", "ctx", None),
        P("head", "ctx", None),
        P("head", "ctx", None),
        P(None, "ctx"),
        P("head", "ctx", None),
    )
    return jax.shard_map(
        per_device,
        mesh=mesh,
        in_specs=placed,
        out_specs=(
            P("head", "ctx", None),
            P("head", "ctx", None),
            P("head", "ctx", None),
            P(None, "ctx"),
        ),
        check_vma=False,
    )
```

```python
import jax
import jax.numpy as jnp
from jax import lax
from jax.experimental import pallas as pl
from jax.experimental.pallas import tpu as pltpu
from jax.sharding import PartitionSpec as P

F32, BF16 = jnp.float32, jnp.bfloat16
NN = (((1,), (0,)), ((), ()))
NT = (((1,), (1,)), ((), ()))
TN = (((0,), (0,)), ((), ()))
VMEM_BYTES = 16 * 2**20
PARTS = (4, 4)
FILL = (1, 2, 0, 2, 0, 2, 0, 1)

INSIDE = pl.BlockSpec(memory_space=pltpu.VMEM)
OUTSIDE = pl.BlockSpec(memory_space=pltpu.HBM)
ANYWHERE = pl.BlockSpec(memory_space=pl.ANY)


def dot(a, b, dims):
    return lax.dot_general(a, b, dims, preferred_element_type=F32)


def block_bits(levels):
    position = lax.axis_index("ctx")
    return [(position >> level & 1) == 1 for level in range(levels)]


def inside(array):
    return pltpu.with_memory_space_constraint(array, pltpu.VMEM)


def outside(array):
    return pltpu.with_memory_space_constraint(array, pltpu.HBM)


def call(kernel, name, args, specs, outs, out_specs, deps=(), aliases=None, scratch=()):
    deps = list(deps)
    count = len(args)
    args = [
        inside(arg) if spec is INSIDE else outside(arg) if spec is OUTSIDE else arg
        for arg, spec in zip(args, specs, strict=True)
    ]

    def body(*refs):
        kernel(*refs[:count], *refs[count + len(deps) :])

    return pl.pallas_call(
        body,
        in_specs=list(specs) + [ANYWHERE] * len(deps),
        out_specs=list(out_specs),
        out_shape=list(outs),
        scratch_shapes=list(scratch),
        input_output_aliases=aliases or {},
        compiler_params=pltpu.CompilerParams(vmem_limit_bytes=VMEM_BYTES),
        cost_estimate=pl.CostEstimate(flops=1, bytes_accessed=1, transcendentals=0),
        name=name,
    )(*args, *deps)


def load_states(pairs, held, first, count, deps):
    shape = pairs[0].shape
    depth = shape[2]
    number = len(pairs)

    def kernel(*refs):
        sems = refs[-1]
        state = refs[-2]
        inner = refs[-2 - number : -2]
        halves = [(0, count // 2), (count // 2, count)] if count > 1 else [(0, 1)]
        copies = []
        for half, (start, stop) in enumerate(halves):
            at = pl.ds(first + start, stop - start)
            for j in range(2):
                copies.append(
                    pltpu.make_async_copy(refs[j].at[at], inner[j].at[at], sems.at[j, half])
                )
        for j in range(2, number):
            copies.append(pltpu.make_async_copy(refs[j], inner[j], sems.at[j, 0]))
        for copy in copies:
            copy.start()
        for half, (start, stop) in enumerate(halves):
            copies[2 * half].wait()
            copies[2 * half + 1].wait()
            for i in range(start, stop):
                state[i] = dot(inner[0][first + i], inner[1][first + i], TN)
        for copy in copies[2 * len(halves) :]:
            copy.wait()

    kind = pltpu.VMEM(shape, BF16)
    return call(
        kernel,
        "load_states",
        [*pairs, *held],
        [OUTSIDE] * number + [INSIDE] * len(held),
        [kind] * number + [jax.ShapeDtypeStruct((count, depth, depth), F32)],
        [INSIDE] * (number + 1),
        deps,
        {number + i: i for i in range(len(held))},
        [pltpu.SemaphoreType.DMA((number, 2))],
    )


def state_grads(queries, out_grad, level_weight, first, count, deps):
    _, length, depth = queries.shape
    levels = level_weight.shape[0] - 1

    def kernel(q_ref, g_ref, w_ref, *outs):
        bits = block_bits(levels)
        for i in range(count):
            turned = g_ref[first + i].T.astype(F32)
            weighted = [
                (keep(bits[level], w_ref[level + 1 : level + 2, :]) * turned).astype(BF16)
                for level in range(levels)
            ]
            grads = dot(jnp.concatenate(weighted, axis=0), q_ref[first + i], NN)
            for level in range(levels):
                outs[level][i] = grads[level * depth : (level + 1) * depth]

    return call(
        kernel,
        "state_grads",
        [queries, out_grad, level_weight],
        [INSIDE] * 3,
        [jax.ShapeDtypeStruct((count, depth, depth), F32)] * levels,
        [INSIDE] * levels,
        deps,
    )


def local_head(level_weight, queries, key_rows, value_rows, out_grad, held, at, deps):
    heads, length, depth = queries.shape
    tile = min(256, length)

    def kernel(w_ref, q_ref, k_ref, v_ref, g_ref, *rest):
        lq_ref, lk_ref, lv_ref, lw_ref = rest[-4:]
        k_turned = k_ref[at].T
        tiles = length // tile

        def products(i):
            upto = (i + 1) * tile
            t = pl.ds(i * tile, tile)
            raw = dot(k_ref[at, :upto, :], q_ref[at, t, :], NT)
            return raw, dot(v_ref[at, :upto, :], g_ref[at, t, :], NT)

        later = products(0)
        for i in range(tiles):
            raw, d_attn = later
            if i + 1 < tiles:
                later = products(i + 1)
            upto = (i + 1) * tile
            t = pl.ds(i * tile, tile)
            w = w_ref[0:1, t]
            rows = lax.broadcasted_iota(jnp.int32, (upto, tile), 0)
            columns = lax.broadcasted_iota(jnp.int32, (upto, tile), 1) + i * tile
            raw = jnp.where(rows <= columns, raw, 0.0)
            d_attn = jnp.where(rows <= columns, d_attn, 0.0)
            lw_ref[0:1, t] = jnp.sum(raw * d_attn, axis=0, keepdims=True)
            attn = (raw * w).astype(BF16)
            d_raw = (d_attn * w).astype(BF16)
            k_part = dot(d_raw, q_ref[at, t, :], NN)
            v_part = dot(attn, g_ref[at, t, :], NN)
            lk_ref[at, t, :] = k_part[i * tile :]
            lv_ref[at, t, :] = v_part[i * tile :]
            if i:
                lk_ref[at, : i * tile, :] += k_part[: i * tile]
                lv_ref[at, : i * tile, :] += v_part[: i * tile]
            lq_ref[at, :, t] = dot(k_turned[:, :upto], d_raw, NN)

    return call(
        kernel,
        "local",
        [level_weight, queries, key_rows, value_rows, out_grad, *held],
        [INSIDE] * (5 + len(held)),
        [
            pltpu.VMEM((heads, depth, length), F32),
            pltpu.VMEM(queries.shape, F32),
            pltpu.VMEM(queries.shape, F32),
            jax.ShapeDtypeStruct((1, length), F32),
        ],
        [INSIDE] * 4,
        deps,
        {5 + i: i for i in range(len(held))},
    )


def mix(levels, arrays, rule, deps):
    def kernel(*refs):
        refs[-1][...] = rule(block_bits(levels), [ref[...] for ref in refs[:-1]])

    return call(
        kernel,
        "mix",
        arrays,
        [INSIDE] * len(arrays),
        [jax.ShapeDtypeStruct(arrays[0].shape, F32)],
        [INSIDE],
        deps,
    )[0]


def keep(flag, array):
    return jnp.where(flag, array, 0.0)


def query_side(level_weight, queries, out_grad, query_sum, states, rows, first, out, done, deps):
    shape = queries.shape
    _, length, depth = shape
    count = states[0].shape[0]
    levels = len(states) - 1
    single, whole = rows

    def kernel(w_ref, q_ref, g_ref, sum_ref, *rest):
        state_refs = rest[: levels + 1]
        singles = rest[levels + 1 : levels + 1 + len(single)]
        wholes = rest[levels + 1 + len(single) : levels + 1 + len(single) + len(whole)]
        if done:
            out_ref, row_ref, far_ref, sem = rest[-4:]
            leave = pltpu.make_async_copy(out_ref.at[:done], far_ref.at[:done], sem)
            leave.start()
        else:
            out_ref, row_ref = rest[-2:]
        bits = block_bits(levels)
        totals = [None] * levels

        def product(i):
            parts = [state_refs[level][i] for level in range(levels)]
            parts[-1] = jnp.where(bits[levels - 2], state_refs[levels][i], parts[-1])
            parts = [keep(bit_here, part).astype(BF16) for bit_here, part in zip(bits, parts, strict=True)]
            return dot(jnp.concatenate(parts, axis=0), g_ref[first + i], NT)

        later = product(0)
        for i in range(count):
            z_all = later
            if i + 1 < count:
                later = product(i + 1)
            turned = q_ref[first + i].T.astype(F32)
            total = sum_ref[first + i]
            for level in range(levels):
                z = z_all[level * depth : (level + 1) * depth]
                total = total + w_ref[level + 1 : level + 2, :] * z
                row = jnp.sum(turned * z, axis=0, keepdims=True)
                totals[level] = row if totals[level] is None else totals[level] + row
            out_ref[first + i] = total.T.astype(BF16)
        own = jnp.zeros((1, length), F32)
        for ref in singles:
            own = own + ref[...]
        for ref in wholes:
            own = own + ref[0:1, :]
            for level in range(levels):
                totals[level] += ref[level + 1 : level + 2, :]
        row_ref[0:1, :] = own
        for level in range(levels):
            row_ref[level + 1 : level + 2, :] = totals[level]
        if done:
            leave.wait()

    args = [level_weight, queries, out_grad, query_sum, *states, *single, *whole]
    return call(
        kernel,
        "query_side",
        args + list(out),
        [INSIDE] * (len(args) + len(out)),
        [pltpu.VMEM(shape, BF16), jax.ShapeDtypeStruct((levels + 1, length), F32)]
        + ([jax.ShapeDtypeStruct(shape, BF16)] if done else []),
        [INSIDE] * 2 + ([OUTSIDE] if done else []),
        deps,
        {len(args): 0} if out else {},
        [pltpu.SemaphoreType.DMA] if done else [],
    )


def key_side(key_rows, value_rows, key_sum, value_sum, parts, levels, rows, first, out, inner, deps):
    shape = key_rows.shape
    _, length, depth = shape
    count = parts[0].shape[0]
    summed = [jax.ShapeDtypeStruct(rows[0].shape, F32)] if rows else []
    moved = list(inner[:2])
    outs = 2 + len(summed) + len(moved) // 2

    def kernel(k_ref, v_ref, ks_ref, vs_ref, *rest):
        k_out, v_out = rest[len(parts) + len(rows) + len(moved) + len(out) :][:2]
        staged, sems = rest[len(parts) + len(rows) + len(moved) + len(out) + outs :][:2]
        bits = block_bits(levels)
        copies = []
        if rows:
            total = rest[len(parts)][...]
            for ref in rest[len(parts) + 1 : len(parts) + len(rows)]:
                total = total + ref[...]
            rest[-2][...] = total
            far_ref = rest[len(parts) + len(rows) + len(moved) + len(out) + 2]
            copies.append(pltpu.make_async_copy(rest[-2], far_ref, rest[-1]))
            copies[0].start()
        if moved:
            span = pl.ds(inner[2], shape[0] - inner[2])
            near_ref = rest[len(parts) + len(rows)]
            far_ref = rest[len(parts) + len(rows) + 2 + len(out) + 2 + len(summed)]
            copies.append(pltpu.make_async_copy(near_ref.at[span], far_ref.at[span], rest[-1]))
            copies[-1].start()

        def products(i):
            grad = gathered(bits, [rest[j][i] for j in range(len(parts))]).astype(BF16)
            return dot(v_ref[first + i], grad, NN), dot(k_ref[first + i], grad, NT)

        later = products(0)
        for i in range(count):
            added = later
            if i + 1 < count:
                later = products(i + 1)
            at = first + i
            for j, (ref, sum_ref) in enumerate(((k_out, ks_ref), (v_out, vs_ref))):
                staged[j, i] = (sum_ref[at] + added[j]).astype(BF16)
                copy = pltpu.make_async_copy(staged.at[j, i], ref.at[at], sems.at[j, i])
                copy.start()
                copies.append(copy)
        for copy in copies:
            copy.wait()

    args = [key_rows, value_rows, key_sum, value_sum, *parts, *rows]
    scratch = [pltpu.VMEM((2, count, length, depth), BF16), pltpu.SemaphoreType.DMA((2, count))]
    if rows:
        scratch.append(pltpu.VMEM(rows[0].shape, F32))
    if rows or moved:
        scratch.append(pltpu.SemaphoreType.DMA)
    aliases = {len(args) + len(moved) + i: i for i in range(len(out))}
    if moved:
        aliases[len(args) + 1] = outs - 1
    return call(
        kernel,
        "key_side",
        args + moved + list(out),
        [INSIDE] * len(args) + ([INSIDE, OUTSIDE] if moved else []) + [OUTSIDE] * len(out),
        [jax.ShapeDtypeStruct(shape, BF16)] * 2
        + summed
        + ([jax.ShapeDtypeStruct(shape, BF16)] if moved else []),
        [OUTSIDE] * outs,
        deps,
        aliases,
        scratch,
    )


def bit(n, level):
    return n >> level & 1


def swaps(size):
    levels = size.bit_length() - 1
    top, low = levels - 1, levels - 2
    up = [[(n, n ^ 2**level) for n in range(size)] for level in range(low)]
    across = [(n, n ^ 2**low) for n in range(size)]
    middle = []
    for n in range(size):
        if bit(n, top) != bit(n, low):
            middle.append((n, n ^ 2**top ^ 2**low))
        else:
            middle.append((n, n ^ 1 if low else size - 1 - n))
    return up + [across, middle, across] + up[::-1]


def gathered(bits, terms):
    top, low = bits[-1], bits[-2]
    total = jnp.where(low, keep(~top, terms[0]), terms[1])
    for term in terms[2:]:
        total = total + term
    return total


def per_device(queries, key_rows, value_rows, level_weight, out_grad):
    size = lax.axis_size("ctx")
    levels = size.bit_length() - 1
    top, low = levels - 1, levels - 2
    heads = queries.shape[0]
    counts = PARTS if sum(PARTS) == heads else (heads - heads // 2, heads // 2)
    parts = range(len(counts))
    firsts = [sum(counts[:part]) for part in parts]
    steps = swaps(size)
    w_in = level_weight
    got, grads, ups = [[] for _ in parts], [None for _ in parts], [None for _ in parts]
    inner, dep = [], []
    for part in parts:
        more = part == parts[-1]
        pairs = [key_rows, value_rows] + ([queries, out_grad] if more else [])
        *inner, state = load_states(pairs, inner, firsts[part], counts[part], dep)
        ups[part] = [state]
        dep = [state]
        if low:
            got[part].append(lax.ppermute(state, "ctx", steps[0]))
    k_in, v_in, q_in, g_in = inner

    held, rows, todo = [], [], list(range(heads))

    def local(dep):
        nonlocal held
        if todo:
            *held, row = local_head(w_in, q_in, k_in, v_in, g_in, held, todo.pop(0), dep)
            rows.append(row)
            dep = [row]
        return dep

    def advance(step, part, dep):
        have, grad = got[part], grads[part]
        if step < low:
            terms = ups[part] + have

            def rule(bits, terms):
                return sum(terms[1:], terms[0])

        elif step == low:
            terms = ups[part] + have + [grad[top]]

            def rule(bits, terms):
                return jnp.where(bits[low], terms[-1], sum(terms[1:-1], terms[0]))

        elif step == low + 1:
            terms = ups[part] + have[:low] + [grad[top], have[low]]

            def rule(bits, terms):
                up = sum(terms[1:-2], terms[0])
                return jnp.where(bits[top], terms[-2], up) + terms[-1]

        elif step == low + 2:
            terms = [grad[low], have[low + 1]]

            def rule(bits, terms):
                other = jnp.where(bits[low], keep(~bits[top], terms[1]), terms[1])
                return keep(bits[low], terms[0]) + other

        else:
            terms = [grad[2 * low + 2 - step], *have[low + 1 :]]

            def rule(bits, terms):
                return terms[0] + gathered(bits, terms[1:])

        sent = mix(levels, terms, rule, dep)
        have.append(lax.ppermute(sent, "ctx", steps[step]))
        return [sent]

    for part in parts:
        grads[part] = state_grads(q_in, g_in, w_in, firsts[part], counts[part], dep)
        dep = [grads[part][top]]

    query_out, weight_rows, far, asked = [], [], [], list(parts)

    def query(dep):
        part = asked.pop(0)
        grad, row, *far[:] = query_side(
            w_in,
            q_in,
            g_in,
            held[0],
            got[part][: levels + 1],
            ([] if asked else rows, weight_rows),
            firsts[part],
            query_out,
            firsts[part],
            dep,
        )
        query_out[:], weight_rows[:] = [grad], [row]
        return [row]

    fill = list(FILL)
    for step in range(1 if low else 0, len(steps)):
        for part in parts:
            if step == low + 3 and part:
                dep = query(dep)
            for _ in range(fill.pop(0) if fill else 0):
                dep = local(dep)
            dep = advance(step, part, dep)
    while todo:
        dep = local(dep)
    while asked:
        dep = query(dep)
    ways = lax.axis_size("head")
    weight_rows += [
        lax.ppermute(weight_rows[0], "head", [(n, (n + shift) % ways) for n in range(ways)])
        for shift in range(1, ways)
    ]
    key_out, query_grad, weight_grad = [], None, None
    for part in parts:
        key_grad, value_grad, *more = key_side(
            k_in,
            v_in,
            held[1],
            held[2],
            got[part][low + 1 :],
            levels,
            weight_rows if part == parts[-1] else [],
            firsts[part],
            key_out,
            (query_out[0], far[0], firsts[-1]) if part == parts[0] else (),
            dep,
        )
        if part == parts[0]:
            query_grad = more.pop()
        if part == parts[-1]:
            weight_grad = more.pop()
        key_out, dep = [key_grad, value_grad], []
    return query_grad, key_out[0], key_out[1], weight_grad


def solution(mesh):
    placed = (
        P("head", "ctx", None),
        P("head", "ctx", None),
        P("head", "ctx", None),
        P(None, "ctx"),
        P("head", "ctx", None),
    )
    return jax.shard_map(
        per_device,
        mesh=mesh,
        in_specs=placed,
        out_specs=(
            P("head", "ctx", None),
            P("head", "ctx", None),
            P("head", "ctx", None),
            P(None, "ctx"),
        ),
        check_vma=False,
    )
```
